256 devices in a mesh: member: 16 (over y, x_lo, core), tp: 16 (over x_hi, z).
Axes of the slice: x: 4 (x_hi: 2, x_lo: 2; x = x_hi * 2 + x_lo), y: 4, z: 8, core: 2. Of those that a mesh axis runs over, the one named last changes fastest.
Arguments:
- source: int32 [16], replicated, may hold values from 0 to 15, as said below
- query_rows: bfloat16 [16, 1024, 4096], P('member', None, 'tp'), may hold values from -6 to 6
- key_rows: bfloat16 [16, 1024, 4096], P('member', None, 'tp'), may hold values from -6 to 6
- value_rows: bfloat16 [16, 1024, 4096], P('member', None, 'tp'), may hold values from -6 to 6
- cotangent: bfloat16 [16, 1024, 2560], P('member', 'tp'), may hold values from -6 to 6
- out_weight: bfloat16 [16, 4096, 2560], P('member', 'tp'), may hold values from -0.09375 to 0.09375
- first_moment: bfloat16 [16, 4096, 2560], P('member', 'tp'), may hold values from -24 to 24
- second_moment: bfloat16 [16, 4096, 2560], P('member', 'tp'), may hold values from 4 to 100
Outputs:
- mixture: bfloat16 [16, 1024, 2560], P('member', 'tp')
- query_grad: bfloat16 [16, 1024, 4096], P('member', None, 'tp')
- key_grad: bfloat16 [16, 1024, 4096], P('member', None, 'tp')
- value_grad: bfloat16 [16, 1024, 4096], P('member', None, 'tp')
- new_weight: bfloat16 [16, 4096, 2560], P('member', 'tp')
- new_first: bfloat16 [16, 4096, 2560], P('member', 'tp')
- new_second: bfloat16 [16, 4096, 2560], P('member', 'tp')
The draws below stay inside these ranges and needn't reach their ends.
Inputs may be any that keep to these rules, and one draw needn't show every extreme that they name: `source`: each entry is the member's own index or the index of one of 4 donor members, which keep their own; 4 members take another's.
All inputs are finite; a program needn't handle non-finite values.
Results may differ from the reference program's by a relative error of at most 0.0096.
Values may be sent and summed in bfloat16 or wider, within the bound.
No kernel may reach another device: no remote copies, remote signals or barrier semaphores. Data moves between devices by JAX's collectives and lax.ppermute only.
A program may use at most 192 MiB of HBM per device.

```python
import math
import jax
import jax.numpy as jnp
from jax import lax

MEMBERS = 16
HEADS = 32
HD = 128
DOUT = 2560
TOK = 1024
ADAM_STEP = 100


def draw_source(key, part):
    key = jax.random.fold_in(key, 11)
    inner_key, pool_key, pick_key = jax.random.split(key, 3)
    quarter = max(MEMBERS // 4, 1)
    others = (1 + jax.random.permutation(inner_key, MEMBERS - 2)).astype(jnp.int32)
    replaced = others[:quarter]
    kept = jnp.concatenate([jnp.array([0, MEMBERS - 1], jnp.int32), others[quarter:]])
    shuffled = kept[jax.random.permutation(pool_key, MEMBERS - quarter)]
    donors = shuffled[:quarter]
    chosen = jax.random.randint(pick_key, (quarter,), 0, quarter)
    counting = jnp.arange(MEMBERS, dtype=jnp.int32)
    return counting.at[replaced].set(donors[chosen]).astype(jnp.int32)


def draw_query_rows(key, part):
    key = jax.random.fold_in(key, 21)
    return jax.random.truncated_normal(key, -6.0, 6.0, (MEMBERS, TOK, HEADS * HD), jnp.float32).astype(jnp.bfloat16)


def draw_key_rows(key, part):
    key = jax.random.fold_in(key, 31)
    return jax.random.truncated_normal(key, -6.0, 6.0, (MEMBERS, TOK, HEADS * HD), jnp.float32).astype(jnp.bfloat16)


def level_of(stream_key, extent, cuts, smallest, largest):
    def one(position, blocks):
        draws = jax.random.uniform(jax.random.fold_in(jax.random.fold_in(stream_key, 6), position), (blocks,), jnp.float32, smallest / len(cuts), largest / len(cuts))
        return jnp.repeat(jnp.exp(draws), extent[position] // blocks).reshape((-1,) + (1,) * (len(extent) - position - 1))

    level = one(*cuts[0])
    for cut in cuts[1:]:
        level = level * one(*cut)
    return level


def noise(key, shape, spread, reach, pieces=(), held_as=jnp.bfloat16):
    loudness = level_of(key, shape, pieces, -0.22, 0.18) if pieces else 1.0
    values = jax.random.normal(key, shape, jnp.float32) * spread * loudness
    return jnp.minimum(jnp.maximum(values, -reach), reach).astype(held_as)


def setup_inputs(seed: int = 0) -> dict:
    streams_of = jax.random.split(jax.random.key(seed), 9)
    source = draw_source(jax.random.fold_in(streams_of[8], 71), 0)
    query_rows = draw_query_rows(jax.random.fold_in(streams_of[8], 71), 0)
    key_rows = draw_key_rows(jax.random.fold_in(streams_of[8], 71), 0)
    value_rows = noise(streams_of[3], (MEMBERS, TOK, HEADS * HD), 1.0, 6.0, ((0, 16), (2, 16)))
    cotangent = noise(streams_of[4], (MEMBERS, TOK, DOUT), 1.0, 6.0, ((0, 16), (1, 16)))
    out_weight = noise(streams_of[5], (MEMBERS, HEADS * HD, DOUT), (HEADS * HD) ** -0.5, 0.09375, ((0, 16), (1, 16)))
    first_moment = noise(streams_of[6], (MEMBERS, HEADS * HD, DOUT), 4.0, 24.0, ((0, 16), (1, 16)))
    second_moment = jnp.clip(jnp.exp(math.log(100.0) - 3.218876 * jax.random.uniform(streams_of[7], (MEMBERS, HEADS * HD, DOUT), jnp.float32) ** level_of(streams_of[7], (MEMBERS, HEADS * HD, DOUT), ((0, 16), (1, 16)), -0.2, 0.2)), 4.0, 100.0).astype(jnp.bfloat16)
    return {"source": source, "query_rows": query_rows, "key_rows": key_rows, "value_rows": value_rows, "cotangent": cotangent, "out_weight": out_weight, "first_moment": first_moment, "second_moment": second_moment}


def attend(query_rows, key_rows, value_rows):
    length = query_rows.shape[0]
    head_count = query_rows.shape[1] // HD
    query_heads = query_rows.reshape(length, head_count, HD).astype(jnp.float32)
    key_heads = key_rows.reshape(length, head_count, HD).astype(jnp.float32)
    value_heads = value_rows.reshape(length, head_count, HD).astype(jnp.float32)
    scores = jnp.einsum('qhd,khd->hqk', query_heads, key_heads) * HD ** (-0.5)
    positions = jnp.arange(length)
    causal = positions[:, None] >= positions[None, :]
    scores = jnp.where(causal[None], scores, -1e+30)
    row_max = lax.optimization_barrier(jnp.max(scores, axis=-1, keepdims=True))
    lifted = jnp.exp(scores - row_max)
    chances = lifted / lax.optimization_barrier(jnp.sum(lifted, axis=-1, keepdims=True))
    rounded = chances.astype(jnp.bfloat16)
    attended = jnp.einsum('hqk,khd->qhd', rounded.astype(jnp.float32), value_heads)
    attended = attended.reshape(length, head_count * HD).astype(jnp.bfloat16)
    return (attended, chances, rounded)

def attend_back(query_rows, key_rows, value_rows, chances, rounded, upstream):
    length = query_rows.shape[0]
    head_count = query_rows.shape[1] // HD
    query_heads = query_rows.reshape(length, head_count, HD).astype(jnp.float32)
    key_heads = key_rows.reshape(length, head_count, HD).astype(jnp.float32)
    value_heads = value_rows.reshape(length, head_count, HD).astype(jnp.float32)
    upstream_heads = upstream.reshape(length, head_count, HD).astype(jnp.float32)
    prob_grad = jnp.einsum('qhd,khd->hqk', upstream_heads, value_heads)
    value_grad = jnp.einsum('hqk,qhd->khd', rounded.astype(jnp.float32), upstream_heads)
    center = lax.optimization_barrier(jnp.sum(chances * prob_grad, axis=-1, keepdims=True))
    score_grad = (chances * (prob_grad - center) * HD ** (-0.5)).astype(jnp.bfloat16)
    query_grad = jnp.einsum('hqk,khd->qhd', score_grad.astype(jnp.float32), key_heads)
    key_grad = jnp.einsum('hqk,qhd->khd', score_grad.astype(jnp.float32), query_heads)
    width = head_count * HD
    return (query_grad.reshape(length, width).astype(jnp.bfloat16), key_grad.reshape(length, width).astype(jnp.bfloat16), value_grad.reshape(length, width).astype(jnp.bfloat16))

def adam(weight, moment_one, moment_two, gradient):
    first_full = 0.9 * moment_one.astype(jnp.float32) + 0.1 * gradient
    second_full = 0.999 * moment_two.astype(jnp.float32) + 0.001 * gradient * gradient
    fix_one = 1.0 - 0.9 ** ADAM_STEP
    fix_two = 1.0 - 0.999 ** ADAM_STEP
    update = first_full / fix_one / (jnp.sqrt(second_full / fix_two) + 1e-08)
    new_weight = (weight.astype(jnp.float32) - 0.001 * update).astype(jnp.bfloat16)
    return (new_weight, first_full.astype(jnp.bfloat16), second_full.astype(jnp.bfloat16))

def reference(source, query_rows, key_rows, value_rows, cotangent, out_weight, first_moment, second_moment):

    def one_member(member):
        anchor = source[member]
        weight = out_weight[anchor]
        moment_one = first_moment[anchor]
        moment_two = second_moment[anchor]
        queries_here = query_rows[member]
        keys_here = key_rows[member]
        values_here = value_rows[member]
        attended, chances, rounded = attend(queries_here, keys_here, values_here)
        mixture = jnp.dot(attended, weight, preferred_element_type=jnp.float32).astype(jnp.bfloat16)
        member_cotangent = cotangent[member]
        upstream = lax.dot_general(member_cotangent, weight, (((1,), (1,)), ((), ())), preferred_element_type=jnp.float32).astype(jnp.bfloat16)
        gradient = lax.dot_general(attended, member_cotangent, (((0,), (0,)), ((), ())), preferred_element_type=jnp.float32)
        query_grad, key_grad, value_grad = attend_back(queries_here, keys_here, values_here, chances, rounded, upstream)
        new_weight, new_first, new_second = adam(weight, moment_one, moment_two, gradient)
        return (mixture, query_grad, key_grad, value_grad, new_weight, new_first, new_second)
    results = lax.map(one_member, jnp.arange(MEMBERS, dtype=jnp.int32))
    return (results[0], results[1], results[2], results[3], results[4], results[5], results[6])
```

```python
import jax
import jax.numpy as jnp
from jax import lax
from jax.experimental import pallas as pl
from jax.experimental.pallas import tpu as pltpu
from jax.sharding import PartitionSpec as P

HD = 128
ADAM_STEP = 100
MEMBERS = 16
ZED = 8
HALVES = 2
TOK = 1024
DOUT = 2560
COLS = 256
CHUNK = TOK // (ZED * HALVES)
QB = 256
SCALE = HD ** (-0.5)
VMEM_BYTES = 48 * 1024 * 1024

Z_GROUPS = [[half * ZED + z for z in range(ZED)] for half in range(HALVES)]
HALF_SWAP = [(t, (t + ZED) % (ZED * HALVES)) for t in range(ZED * HALVES)]

NN = (((1,), (0,)), ((), ()))
NT = (((1,), (1,)), ((), ()))


def mm(a, b, dims):
    return lax.dot_general(a, b, dims, preferred_element_type=jnp.float32)


def params(**more):
    return pltpu.CompilerParams(vmem_limit_bytes=VMEM_BYTES, **more)


def cost(flops, nbytes, trans=0):
    return pl.CostEstimate(flops=flops, bytes_accessed=nbytes, transcendentals=trans)


def place(t):
    return (t % ZED) * HALVES + t // ZED


def forward_kernel(q_ref, k_ref, v_ref, att_ref, p_ref):
    keys = k_ref[...]
    values_t = v_ref[...].astype(jnp.float32).T.astype(jnp.bfloat16)
    row = lax.broadcasted_iota(jnp.int32, (QB, QB), 0)
    col = lax.broadcasted_iota(jnp.int32, (QB, QB), 1)
    visible = row <= col
    for i in range(TOK // QB):
        low, high = i * QB, (i + 1) * QB
        queries = q_ref[low:high, :]
        last = jnp.where(visible, mm(keys[low:high], queries, NT) * SCALE, -1e30)
        top = jnp.max(last, axis=0, keepdims=True)
        if i:
            early = mm(keys[:low], queries, NT) * SCALE
            top = jnp.maximum(top, jnp.max(early, axis=0, keepdims=True))
            early = jnp.exp(early - top)
        last = jnp.exp(last - top)
        total = jnp.sum(last, axis=0, keepdims=True)
        if i:
            total = total + jnp.sum(early, axis=0, keepdims=True)
        inverse = 1.0 / total
        last = (last * inverse).astype(jnp.bfloat16)
        p_ref[0, low:high, low:high] = last
        out_t = mm(values_t[:, low:high], last, NN)
        if i:
            early = (early * inverse).astype(jnp.bfloat16)
            p_ref[0, :low, low:high] = early
            out_t = out_t + mm(values_t[:, :low], early, NN)
        rows = out_t.T.astype(jnp.bfloat16)
        for part in range(QB // CHUNK):
            att_ref[place(i * (QB // CHUNK) + part)] = rows[part * CHUNK : (part + 1) * CHUNK]


def forward(queries, keys, values):
    heads = COLS // HD
    head_block = pl.BlockSpec((TOK, HD), lambda h: (0, h))
    return pl.pallas_call(
        forward_kernel,
        grid=(heads,),
        in_specs=[head_block] * 3,
        out_specs=[
            pl.BlockSpec((ZED * HALVES, CHUNK, HD), lambda h: (0, 0, h)),
            pl.BlockSpec((1, TOK, TOK), lambda h: (h, 0, 0)),
        ],
        out_shape=[
            jax.ShapeDtypeStruct((ZED * HALVES, CHUNK, COLS), jnp.bfloat16),
            jax.ShapeDtypeStruct((heads, TOK, TOK), jnp.bfloat16),
        ],
        compiler_params=params(),
        cost_estimate=cost(4 * TOK * TOK * COLS, 8 * TOK * COLS + 2 * heads * TOK * TOK, heads * TOK * TOK),
        name="attend_forward",
    )(queries, keys, values)


def project_kernel(a_ref, w_ref, o_ref):
    o_ref[...] = mm(a_ref[...], w_ref[...], NN).astype(jnp.bfloat16)


def project(attended, weight):
    block = 256
    return pl.pallas_call(
        project_kernel,
        grid=(TOK // block,),
        in_specs=[
            pl.BlockSpec((block, COLS), lambda i: (i, 0)),
            pl.BlockSpec((COLS, DOUT), lambda i: (0, 0)),
        ],
        out_specs=pl.BlockSpec((block, DOUT), lambda i: (i, 0)),
        out_shape=jax.ShapeDtypeStruct((TOK, DOUT), jnp.bfloat16),
        compiler_params=params(),
        cost_estimate=cost(2 * TOK * COLS * DOUT, 2 * (TOK * COLS + COLS * DOUT + TOK * DOUT)),
        name="project",
    )(attended, weight)


def gradient_kernel(a_ref, c_ref, o_ref, t_ref):
    @pl.when(pl.program_id(0) == 0)
    def _():
        t_ref[...] = a_ref[...].astype(jnp.float32).T.astype(jnp.bfloat16)

    o_ref[...] = mm(t_ref[...], c_ref[...], NN)


def gradient_of(attended, incoming):
    block = 512
    return pl.pallas_call(
        gradient_kernel,
        grid=(DOUT // block,),
        in_specs=[
            pl.BlockSpec((TOK, COLS), lambda i: (0, 0)),
            pl.BlockSpec((TOK, block), lambda i: (0, i)),
        ],
        out_specs=pl.BlockSpec((COLS, block), lambda i: (0, i)),
        out_shape=jax.ShapeDtypeStruct((COLS, DOUT), jnp.float32),
        scratch_shapes=[pltpu.VMEM((COLS, TOK), jnp.bfloat16)],
        compiler_params=params(),
        cost_estimate=cost(2 * TOK * COLS * DOUT, 2 * TOK * (COLS + DOUT) + 4 * COLS * DOUT),
        name="weight_gradient",
    )(attended, incoming)


def backward_kernel(c_ref, w_ref, q_ref, k_ref, v_ref, p_ref, dq_ref, dk_ref, dv_ref, u_ref, ak_ref, av_ref):
    head = pl.program_id(0)

    @pl.when(head == 0)
    def _():
        step = 256
        for block in range(TOK // step):
            rows = mm(c_ref[block * step : (block + 1) * step, :], w_ref[...], NT).astype(jnp.bfloat16)
            for part in range(step // CHUNK):
                spot = block * (step // CHUNK) + part
                t = (spot % HALVES) * ZED + spot // HALVES
                for h in range(COLS // HD):
                    u_ref[h, t * CHUNK : (t + 1) * CHUNK, :] = rows[
                        part * CHUNK : (part + 1) * CHUNK, h * HD : (h + 1) * HD
                    ]

    keys_t = k_ref[...].astype(jnp.float32).T.astype(jnp.bfloat16)
    blocks = TOK // QB
    for i in reversed(range(blocks)):
        low, high = i * QB, (i + 1) * QB
        up = u_ref[head, low:high, :]
        chance = p_ref[0, :high, low:high]
        wide = chance.astype(jnp.float32)
        prob_grad = mm(v_ref[:high, :], up, NT)
        center = jnp.sum(wide * prob_grad, axis=0, keepdims=True)
        score_grad = (wide * (prob_grad - center) * SCALE).astype(jnp.bfloat16)
        dq_ref[low:high, :] = mm(keys_t[:, :high], score_grad, NN).T.astype(jnp.bfloat16)
        more_v = mm(chance, up, NN)
        more_k = mm(score_grad, q_ref[low:high, :], NN)
        if i == blocks - 1:
            av_ref[...] = more_v
            ak_ref[...] = more_k
        else:
            av_ref[:high, :] += more_v
            ak_ref[:high, :] += more_k
    dv_ref[...] = av_ref[...].astype(jnp.bfloat16)
    dk_ref[...] = ak_ref[...].astype(jnp.bfloat16)


def backward(incoming, weight, queries, keys, values, chances):
    heads = COLS // HD
    head_block = pl.BlockSpec((TOK, HD), lambda h: (0, h))
    return pl.pallas_call(
        backward_kernel,
        grid=(heads,),
        in_specs=[
            pl.BlockSpec((TOK, DOUT), lambda h: (0, 0)),
            pl.BlockSpec((COLS, DOUT), lambda h: (0, 0)),
            head_block,
            head_block,
            head_block,
            pl.BlockSpec((1, TOK, TOK), lambda h: (h, 0, 0)),
        ],
        out_specs=[head_block] * 3,
        out_shape=[jax.ShapeDtypeStruct((TOK, COLS), jnp.bfloat16)] * 3,
        scratch_shapes=[
            pltpu.VMEM((heads, TOK, HD), jnp.bfloat16),
            pltpu.VMEM((TOK, HD), jnp.float32),
            pltpu.VMEM((TOK, HD), jnp.float32),
        ],
        compiler_params=params(),
        cost_estimate=cost(
            2 * TOK * COLS * DOUT + 8 * TOK * TOK * COLS, 2 * (TOK * DOUT + COLS * DOUT + 6 * TOK * COLS + heads * TOK * TOK)
        ),
        name="attend_backward",
    )(incoming, weight, queries, keys, values, chances)


def adam_kernel(w_ref, one_ref, two_ref, g_ref, nw_ref, n1_ref, n2_ref):
    shape = g_ref.shape
    gradient = g_ref[...]
    first_full = 0.9 * one_ref[...].reshape(shape).astype(jnp.float32) + 0.1 * gradient
    second_full = 0.999 * two_ref[...].reshape(shape).astype(jnp.float32) + 0.001 * gradient * gradient
    fix_one = 1.0 - 0.9**ADAM_STEP
    fix_two = 1.0 - 0.999**ADAM_STEP
    update = first_full / fix_one / (jnp.sqrt(second_full / fix_two) + 1e-08)
    nw_ref[...] = (w_ref[...].astype(jnp.float32) - 0.001 * update).astype(jnp.bfloat16)
    n1_ref[...] = first_full.astype(jnp.bfloat16)
    n2_ref[...] = second_full.astype(jnp.bfloat16)


def adam(weight, moments, gradient):
    piece = COLS // MEMBERS
    group = 2
    rows = pl.BlockSpec((group * piece, DOUT), lambda i: (i, 0))
    out = jax.ShapeDtypeStruct((COLS, DOUT), jnp.bfloat16)
    return pl.pallas_call(
        adam_kernel,
        grid=(MEMBERS // group,),
        in_specs=[
            rows,
            pl.BlockSpec((group, piece, DOUT), lambda i: (i, 0, 0)),
            pl.BlockSpec((group, piece, DOUT), lambda i: (i, 1, 0)),
            rows,
        ],
        out_specs=[rows] * 3,
        out_shape=[out] * 3,
        compiler_params=params(),
        cost_estimate=cost(20 * COLS * DOUT, 16 * COLS * DOUT, 3 * COLS * DOUT),
        name="adam",
    )(weight, moments, moments, gradient)


def select_kernel(source_ref, x_ref, o_ref, sems):
    copies = [
        pltpu.make_async_copy(x_ref.at[source_ref[i]], o_ref.at[i], sems.at[i]) for i in range(MEMBERS)
    ]
    for copy in copies:
        copy.start()
    for copy in copies:
        copy.wait()


def select(source, pieces):
    return pl.pallas_call(
        select_kernel,
        in_specs=[pl.BlockSpec(memory_space=pltpu.SMEM), pl.BlockSpec(memory_space=pl.ANY)],
        out_specs=pl.BlockSpec(memory_space=pl.ANY),
        out_shape=jax.ShapeDtypeStruct(pieces.shape, pieces.dtype),
        scratch_shapes=[pltpu.SemaphoreType.DMA((MEMBERS,))],
        compiler_params=params(),
        cost_estimate=cost(0, 4 * pieces.size),
        name="select_pieces",
    )(source, pieces)


def swap_members(pieces):
    return lax.all_to_all(pieces, "member", split_axis=0, concat_axis=0, tiled=True)


def on_device(
    source, query_rows, key_rows, value_rows, cotangent, out_weight, first_moment, second_moment
):
    queries, keys, values = query_rows[0], key_rows[0], value_rows[0]
    half = lax.axis_index("tp") // ZED
    pieces = (MEMBERS, COLS // MEMBERS, DOUT)

    weight = swap_members(select(source, swap_members(out_weight.reshape(pieces)))).reshape(COLS, DOUT)

    own = cotangent[0]
    other = lax.ppermute(own, "tp", HALF_SWAP)
    pair = jnp.where(half == 0, jnp.stack([own, other]), jnp.stack([other, own]))
    incoming = lax.all_gather(
        pair.reshape(HALVES * CHUNK, DOUT), "tp", axis=0, tiled=True, axis_index_groups=Z_GROUPS
    )

    attended, chances = forward(queries, keys, values)
    attended = attended.reshape(TOK, COLS)

    partial = project(attended, weight)
    summed = lax.psum_scatter(
        partial, "tp", scatter_dimension=0, tiled=True, axis_index_groups=Z_GROUPS
    ).reshape(HALVES, CHUNK, DOUT)
    mine = lax.dynamic_index_in_dim(summed, half, 0, keepdims=False)
    theirs = lax.ppermute(
        lax.dynamic_index_in_dim(summed, 1 - half, 0, keepdims=False), "tp", HALF_SWAP
    )
    mixture = (mine.astype(jnp.float32) + theirs.astype(jnp.float32)).astype(jnp.bfloat16)

    gradient = gradient_of(attended, incoming)
    query_grad, key_grad, value_grad = backward(incoming, weight, queries, keys, values, chances)

    moments = jnp.concatenate([first_moment.reshape(pieces), second_moment.reshape(pieces)], axis=1)
    moments = swap_members(select(source, swap_members(moments)))
    new_weight, new_first, new_second = adam(weight, moments, gradient)
    return (
        mixture[None],
        query_grad[None],
        key_grad[None],
        value_grad[None],
        new_weight[None],
        new_first[None],
        new_second[None],
    )


def solution(mesh):
    placed = (
        P(),
        P("member", None, "tp"),
        P("member", None, "tp"),
        P("member", None, "tp"),
        P("member", "tp", None),
        P("member", "tp", None),
        P("member", "tp", None),
        P("member", "tp", None),
    )
    return jax.shard_map(
        on_device,
        mesh=mesh,
        in_specs=placed,
        out_specs=(
            P("member", "tp", None),
            P("member", None, "tp"),
            P("member", None, "tp"),
            P("member", None, "tp"),
            P("member", "tp", None),
            P("member", "tp", None),
            P("member", "tp", None),
        ),
        check_vma=False,
    )
```

```python
import jax
import jax.numpy as jnp
from jax import lax
from jax.experimental import pallas as pl
from jax.experimental.pallas import tpu as pltpu
from jax.sharding import PartitionSpec as P

HD = 128
ADAM_STEP = 100
MEMBERS = 16
ZED = 8
HALVES = 2
TOK = 1024
DOUT = 2560
COLS = 256
CHUNK = TOK // (ZED * HALVES)
QB = 256
SCALE = HD ** (-0.5)
VMEM_BYTES = 48 * 1024 * 1024

Z_GROUPS = [[half * ZED + z for z in range(ZED)] for half in range(HALVES)]
PAIRS = [[half * ZED + z for half in range(HALVES)] for z in range(ZED)]
HALF_SWAP = [(t, (t + ZED) % (ZED * HALVES)) for t in range(ZED * HALVES)]

NN = (((1,), (0,)), ((), ()))
NT = (((1,), (1,)), ((), ()))


def mm(a, b, dims):
    return lax.dot_general(a, b, dims, preferred_element_type=jnp.float32)


def params(**more):
    return pltpu.CompilerParams(vmem_limit_bytes=VMEM_BYTES, **more)


def cost(flops, nbytes, trans=0):
    return pl.CostEstimate(flops=flops, bytes_accessed=nbytes, transcendentals=trans)


def place(t):
    return (t % ZED) * HALVES + t // ZED


def forward_kernel(q_ref, k_ref, v_ref, att_ref, p_ref):
    keys = k_ref[...]
    values_t = v_ref[...].astype(jnp.float32).T.astype(jnp.bfloat16)
    row = lax.broadcasted_iota(jnp.int32, (QB, QB), 0)
    col = lax.broadcasted_iota(jnp.int32, (QB, QB), 1)
    visible = row <= col
    for i in range(TOK // QB):
        low, high = i * QB, (i + 1) * QB
        queries = q_ref[low:high, :]
        last = jnp.where(visible, mm(keys[low:high], queries, NT) * SCALE, -1e30)
        top = jnp.max(last, axis=0, keepdims=True)
        if i:
            early = mm(keys[:low], queries, NT) * SCALE
            top = jnp.maximum(top, jnp.max(early, axis=0, keepdims=True))
            early = jnp.exp(early - top)
        last = jnp.exp(last - top)
        total = jnp.sum(last, axis=0, keepdims=True)
        if i:
            total = total + jnp.sum(early, axis=0, keepdims=True)
        inverse = 1.0 / total
        last = (last * inverse).astype(jnp.bfloat16)
        p_ref[0, low:high, low:high] = last
        out_t = mm(values_t[:, low:high], last, NN)
        if i:
            early = (early * inverse).astype(jnp.bfloat16)
            p_ref[0, :low, low:high] = early
            out_t = out_t + mm(values_t[:, :low], early, NN)
        rows = out_t.T.astype(jnp.bfloat16)
        for part in range(QB // CHUNK):
            att_ref[place(i * (QB // CHUNK) + part)] = rows[part * CHUNK : (part + 1) * CHUNK]


def forward(queries, keys, values):
    heads = COLS // HD
    head_block = pl.BlockSpec((TOK, HD), lambda h: (0, h))
    return pl.pallas_call(
        forward_kernel,
        grid=(heads,),
        in_specs=[head_block] * 3,
        out_specs=[
            pl.BlockSpec((ZED * HALVES, CHUNK, HD), lambda h: (0, 0, h)),
            pl.BlockSpec((1, TOK, TOK), lambda h: (h, 0, 0)),
        ],
        out_shape=[
            jax.ShapeDtypeStruct((ZED * HALVES, CHUNK, COLS), jnp.bfloat16),
            jax.ShapeDtypeStruct((heads, TOK, TOK), jnp.bfloat16),
        ],
        compiler_params=params(),
        cost_estimate=cost(4 * TOK * TOK * COLS, 8 * TOK * COLS + 2 * heads * TOK * TOK, heads * TOK * TOK),
        name="attend_forward",
    )(queries, keys, values)


def project_kernel(a_ref, w_ref, o_ref):
    o_ref[...] = mm(a_ref[...], w_ref[...], NN).astype(jnp.bfloat16)


def project(attended, weight):
    block = 256
    return pl.pallas_call(
        project_kernel,
        grid=(TOK // block,),
        in_specs=[
            pl.BlockSpec((block, COLS), lambda i: (i, 0)),
            pl.BlockSpec((COLS, DOUT), lambda i: (0, 0)),
        ],
        out_specs=pl.BlockSpec((block, DOUT), lambda i: (i, 0)),
        out_shape=jax.ShapeDtypeStruct((TOK, DOUT), jnp.bfloat16),
        compiler_params=params(),
        cost_estimate=cost(2 * TOK * COLS * DOUT, 2 * (TOK * COLS + COLS * DOUT + TOK * DOUT)),
        name="project",
    )(attended, weight)


def gradient_kernel(a_ref, c_ref, o_ref, t_ref):
    @pl.when(pl.program_id(0) == 0)
    def _():
        t_ref[...] = a_ref[...].astype(jnp.float32).T.astype(jnp.bfloat16)

    o_ref[...] = mm(t_ref[...], c_ref[...], NN)


def gradient_of(attended, incoming):
    block = 512
    return pl.pallas_call(
        gradient_kernel,
        grid=(DOUT // block,),
        in_specs=[
            pl.BlockSpec((TOK, COLS), lambda i: (0, 0)),
            pl.BlockSpec((TOK, block), lambda i: (0, i)),
        ],
        out_specs=pl.BlockSpec((COLS, block), lambda i: (0, i)),
        out_shape=jax.ShapeDtypeStruct((COLS, DOUT), jnp.float32),
        scratch_shapes=[pltpu.VMEM((COLS, TOK), jnp.bfloat16)],
        compiler_params=params(),
        cost_estimate=cost(2 * TOK * COLS * DOUT, 2 * TOK * (COLS + DOUT) + 4 * COLS * DOUT),
        name="weight_gradient",
    )(attended, incoming)


def backward_kernel(c_ref, w_ref, q_ref, k_ref, v_ref, p_ref, dq_ref, dk_ref, dv_ref, u_ref, ak_ref, av_ref):
    head = pl.program_id(0)

    @pl.when(head == 0)
    def _():
        step = 256
        for block in range(TOK // step):
            rows = mm(c_ref[block * step : (block + 1) * step, :], w_ref[...], NT).astype(jnp.bfloat16)
            for part in range(step // CHUNK):
                spot = block * (step // CHUNK) + part
                t = (spot % HALVES) * ZED + spot // HALVES
                for h in range(COLS // HD):
                    u_ref[h, t * CHUNK : (t + 1) * CHUNK, :] = rows[
                        part * CHUNK : (part + 1) * CHUNK, h * HD : (h + 1) * HD
                    ]

    keys_t = k_ref[...].astype(jnp.float32).T.astype(jnp.bfloat16)
    blocks = TOK // QB
    for i in reversed(range(blocks)):
        low, high = i * QB, (i + 1) * QB
        up = u_ref[head, low:high, :]
        chance = p_ref[0, :high, low:high]
        wide = chance.astype(jnp.float32)
        prob_grad = mm(v_ref[:high, :], up, NT)
        center = jnp.sum(wide * prob_grad, axis=0, keepdims=True)
        score_grad = (wide * (prob_grad - center) * SCALE).astype(jnp.bfloat16)
        dq_ref[low:high, :] = mm(keys_t[:, :high], score_grad, NN).T.astype(jnp.bfloat16)
        more_v = mm(chance, up, NN)
        more_k = mm(score_grad, q_ref[low:high, :], NN)
        if i == blocks - 1:
            av_ref[...] = more_v
            ak_ref[...] = more_k
        else:
            av_ref[:high, :] += more_v
            ak_ref[:high, :] += more_k
    dv_ref[...] = av_ref[...].astype(jnp.bfloat16)
    dk_ref[...] = ak_ref[...].astype(jnp.bfloat16)


def backward(incoming, weight, queries, keys, values, chances):
    heads = COLS // HD
    head_block = pl.BlockSpec((TOK, HD), lambda h: (0, h))
    return pl.pallas_call(
        backward_kernel,
        grid=(heads,),
        in_specs=[
            pl.BlockSpec((TOK, DOUT), lambda h: (0, 0)),
            pl.BlockSpec((COLS, DOUT), lambda h: (0, 0)),
            head_block,
            head_block,
            head_block,
            pl.BlockSpec((1, TOK, TOK), lambda h: (h, 0, 0)),
        ],
        out_specs=[head_block] * 3,
        out_shape=[jax.ShapeDtypeStruct((TOK, COLS), jnp.bfloat16)] * 3,
        scratch_shapes=[
            pltpu.VMEM((heads, TOK, HD), jnp.bfloat16),
            pltpu.VMEM((TOK, HD), jnp.float32),
            pltpu.VMEM((TOK, HD), jnp.float32),
        ],
        compiler_params=params(),
        cost_estimate=cost(
            2 * TOK * COLS * DOUT + 8 * TOK * TOK * COLS, 2 * (TOK * DOUT + COLS * DOUT + 6 * TOK * COLS + heads * TOK * TOK)
        ),
        name="attend_backward",
    )(incoming, weight, queries, keys, values, chances)


def adam_kernel(w_ref, one_ref, two_ref, g_ref, nw_ref, n1_ref, n2_ref):
    shape = g_ref.shape
    gradient = g_ref[...]
    first_full = 0.9 * one_ref[...].reshape(shape).astype(jnp.float32) + 0.1 * gradient
    second_full = 0.999 * two_ref[...].reshape(shape).astype(jnp.float32) + 0.001 * gradient * gradient
    fix_one = 1.0 - 0.9**ADAM_STEP
    fix_two = 1.0 - 0.999**ADAM_STEP
    spread = second_full * (1.0 / fix_two)
    update = first_full * (0.001 / fix_one) / (spread * lax.rsqrt(spread) + 1e-08)
    nw_ref[...] = (w_ref[...].astype(jnp.float32) - update).astype(jnp.bfloat16)
    n1_ref[...] = first_full.astype(jnp.bfloat16)
    n2_ref[...] = second_full.astype(jnp.bfloat16)


def adam(weight, moments, gradient):
    piece = COLS // MEMBERS
    group = 8
    rows = pl.BlockSpec((group * piece, DOUT), lambda i: (i, 0))
    out = jax.ShapeDtypeStruct((COLS, DOUT), jnp.bfloat16)
    return pl.pallas_call(
        adam_kernel,
        grid=(MEMBERS // group,),
        in_specs=[
            rows,
            pl.BlockSpec((group, piece, DOUT), lambda i: (i, 0, 0)),
            pl.BlockSpec((group, piece, DOUT), lambda i: (i, 1, 0)),
            rows,
        ],
        out_specs=[rows] * 3,
        out_shape=[out] * 3,
        compiler_params=params(),
        cost_estimate=cost(20 * COLS * DOUT, 16 * COLS * DOUT, 3 * COLS * DOUT),
        name="adam",
    )(weight, moments, moments, gradient)


def select_kernel(source_ref, x_ref, o_ref, sems):
    copies = [
        pltpu.make_async_copy(x_ref.at[source_ref[i]], o_ref.at[i], sems.at[i]) for i in range(MEMBERS)
    ]
    for copy in copies:
        copy.start()
    for copy in copies:
        copy.wait()


def select(source, pieces):
    return pl.pallas_call(
        select_kernel,
        in_specs=[pl.BlockSpec(memory_space=pltpu.SMEM), pl.BlockSpec(memory_space=pl.ANY)],
        out_specs=pl.BlockSpec(memory_space=pl.ANY),
        out_shape=jax.ShapeDtypeStruct(pieces.shape, pieces.dtype),
        scratch_shapes=[pltpu.SemaphoreType.DMA((MEMBERS,))],
        compiler_params=params(),
        cost_estimate=cost(0, 4 * pieces.size),
        name="select_pieces",
    )(source, pieces)


def swap_members(pieces):
    return lax.all_to_all(pieces, "member", split_axis=0, concat_axis=0, tiled=True)


def on_device(
    source, query_rows, key_rows, value_rows, cotangent, out_weight, first_moment, second_moment
):
    queries, keys, values = query_rows[0], key_rows[0], value_rows[0]
    half = lax.axis_index("tp") // ZED
    pieces = (MEMBERS, COLS // MEMBERS, DOUT)

    weight = swap_members(select(source, swap_members(out_weight.reshape(pieces)))).reshape(COLS, DOUT)

    pair = lax.all_gather(cotangent[0], "tp", axis=0, tiled=True, axis_index_groups=PAIRS)
    incoming = lax.all_gather(pair, "tp", axis=0, tiled=True, axis_index_groups=Z_GROUPS)

    attended, chances = forward(queries, keys, values)
    attended = attended.reshape(TOK, COLS)

    partial = project(attended, weight)
    gradient = gradient_of(attended, incoming)
    query_grad, key_grad, value_grad = backward(incoming, weight, queries, keys, values, chances)
    summed = lax.psum_scatter(
        partial, "tp", scatter_dimension=0, tiled=True, axis_index_groups=Z_GROUPS
    ).reshape(HALVES, CHUNK, DOUT)
    summed, query_grad, gradient = lax.optimization_barrier((summed, query_grad, gradient))
    mine = lax.dynamic_index_in_dim(summed, half, 0, keepdims=False)
    theirs = lax.ppermute(
        lax.dynamic_index_in_dim(summed, 1 - half, 0, keepdims=False), "tp", HALF_SWAP
    )
    mixture = (mine.astype(jnp.float32) + theirs.astype(jnp.float32)).astype(jnp.bfloat16)

    moments = jnp.concatenate([first_moment.reshape(pieces), second_moment.reshape(pieces)], axis=1)
    moments = swap_members(select(source, swap_members(moments)))
    new_weight, new_first, new_second = adam(weight, moments, gradient)
    return (
        mixture[None],
        query_grad[None],
        key_grad[None],
        value_grad[None],
        new_weight[None],
        new_first[None],
        new_second[None],
    )


def solution(mesh):
    placed = (
        P(),
        P("member", None, "tp"),
        P("member", None, "tp"),
        P("member", None, "tp"),
        P("member", "tp", None),
        P("member", "tp", None),
        P("member", "tp", None),
        P("member", "tp", None),
    )
    return jax.shard_map(
        on_device,
        mesh=mesh,
        in_specs=placed,
        out_specs=(
            P("member", "tp", None),
            P("member", None, "tp"),
            P("member", None, "tp"),
            P("member", None, "tp"),
            P("member", "tp", None),
            P("member", "tp", None),
            P("member", "tp", None),
        ),
        check_vma=False,
    )
```

```python
import jax
import jax.numpy as jnp
from jax import lax
from jax.experimental import pallas as pl
from jax.experimental.pallas import tpu as pltpu
from jax.sharding import PartitionSpec as P

HD = 128
ADAM_STEP = 100
MEMBERS = 16
ZED = 8
HALVES = 2
TOK = 1024
DOUT = 2560
COLS = 256
CHUNK = TOK // (ZED * HALVES)
QB = 256
SCALE = HD ** (-0.5)
VMEM_BYTES = 48 * 1024 * 1024
ANYWHERE = pl.BlockSpec(memory_space=pl.ANY)

Z_GROUPS = [[half * ZED + z for z in range(ZED)] for half in range(HALVES)]
ORDER = [0, 7, 1, 6, 2, 5, 3, 4]
HALF_SWAP = [(t, (t + ZED) % (ZED * HALVES)) for t in range(ZED * HALVES)]

NN = (((1,), (0,)), ((), ()))
NT = (((1,), (1,)), ((), ()))


def mm(a, b, dims):
    return lax.dot_general(a, b, dims, preferred_element_type=jnp.float32)


def params(vmem=VMEM_BYTES):
    return pltpu.CompilerParams(vmem_limit_bytes=vmem)


def cost(flops, nbytes, trans=0):
    return pl.CostEstimate(flops=flops, bytes_accessed=nbytes, transcendentals=trans)


def ring(step):
    return [(h * ZED + z, h * ZED + (z + step) % ZED) for h in range(HALVES) for z in range(ZED)]


def token_block(z, part, spot_ref):
    half = spot_ref[1]
    return z + ZED * (half + part - 2 * half * part)


def forward_kernel(spot_ref, q_ref, k_ref, v_ref, *refs):
    att_ref, p_ref = refs[-2:]
    half = spot_ref[1]
    keys = k_ref[...]
    values_t = v_ref[...].astype(jnp.float32).T.astype(jnp.bfloat16)
    row = lax.broadcasted_iota(jnp.int32, (QB, QB), 0)
    col = lax.broadcasted_iota(jnp.int32, (QB, QB), 1)
    visible = row <= col
    for i in range(TOK // QB):
        low, high = i * QB, (i + 1) * QB
        queries = q_ref[low:high, :]
        last = jnp.where(visible, mm(keys[low:high], queries, NT) * SCALE, -1e30)
        top = jnp.max(last, axis=0, keepdims=True)
        if i:
            early = mm(keys[:low], queries, NT) * SCALE
            top = jnp.maximum(top, jnp.max(early, axis=0, keepdims=True))
            early = jnp.exp(early - top)
        last = jnp.exp(last - top)
        total = jnp.sum(last, axis=0, keepdims=True)
        if i:
            total = total + jnp.sum(early, axis=0, keepdims=True)
        inverse = 1.0 / total
        last = (last * inverse).astype(jnp.bfloat16)
        p_ref[0, low:high, low:high] = last
        out_t = mm(values_t[:, low:high], last, NN)
        if i:
            early = (early * inverse).astype(jnp.bfloat16)
            p_ref[0, :low, low:high] = early
            out_t = out_t + mm(values_t[:, :low], early, NN)
        rows = out_t.T.astype(jnp.bfloat16)
        for part in range(QB // CHUNK):
            t = i * (QB // CHUNK) + part
            side = half if t < ZED else 1 - half
            att_ref[(t % ZED) * HALVES + side] = rows[part * CHUNK : (part + 1) * CHUNK]


def forward(spot, queries, keys, values, after):
    heads = COLS // HD
    head_block = pl.BlockSpec((TOK, HD), lambda h: (0, h))
    return pl.pallas_call(
        forward_kernel,
        grid=(heads,),
        in_specs=[pl.BlockSpec(memory_space=pltpu.SMEM)] + [head_block] * 3 + [ANYWHERE] * len(after),
        out_specs=[
            pl.BlockSpec((ZED * HALVES, CHUNK, HD), lambda h: (0, 0, h)),
            pl.BlockSpec((1, TOK, TOK), lambda h: (h, 0, 0)),
        ],
        out_shape=[
            jax.ShapeDtypeStruct((ZED * HALVES, CHUNK, COLS), jnp.bfloat16),
            jax.ShapeDtypeStruct((heads, TOK, TOK), jnp.bfloat16),
        ],
        compiler_params=params(),
        cost_estimate=cost(4 * TOK * TOK * COLS, 8 * TOK * COLS + 2 * heads * TOK * TOK, heads * TOK * TOK),
        name="attend_forward",
    )(spot, queries, keys, values, *after)


def project_kernel(a_ref, w_ref, *refs):
    o_ref = refs[-1]
    o_ref[...] = mm(a_ref[...], w_ref[...], NN).astype(jnp.bfloat16)


def project(attended, weight, after):
    block = 256
    return pl.pallas_call(
        project_kernel,
        grid=(TOK // block,),
        in_specs=[
            pl.BlockSpec((block, COLS), lambda i: (i, 0)),
            pl.BlockSpec((COLS, DOUT), lambda i: (0, 0)),
        ]
        + [ANYWHERE] * len(after),
        out_specs=pl.BlockSpec((block, DOUT), lambda i: (i, 0)),
        out_shape=jax.ShapeDtypeStruct((TOK, DOUT), jnp.bfloat16),
        compiler_params=params(),
        cost_estimate=cost(2 * TOK * COLS * DOUT, 2 * (TOK * COLS + COLS * DOUT + TOK * DOUT)),
        name="project",
    )(attended, weight, *after)


def rows_at(place, own_ref, cot_refs, spot_ref):
    z = lax.rem(spot_ref[0] + ORDER[place], ZED)
    return [own_ref[z], cot_refs[place][...]]


def gradient_kernel(spot_ref, a_ref, own_ref, *refs):
    cot_refs, (o_ref, t_ref) = refs[: len(ORDER)], refs[len(ORDER) :]

    @pl.when(pl.program_id(0) == 0)
    def _():
        for place, offset in enumerate(ORDER):
            z = lax.rem(spot_ref[0] + offset, ZED)
            rows = a_ref[pl.ds(z * HALVES, HALVES)].reshape(HALVES * CHUNK, COLS)
            t_ref[:, place * HALVES * CHUNK : (place + 1) * HALVES * CHUNK] = (
                rows.astype(jnp.float32).T.astype(jnp.bfloat16)
            )

    total = None
    width = 2 * HALVES * CHUNK
    for pair in range(len(ORDER) // 2):
        rows = jnp.concatenate(
            [r for place in (2 * pair, 2 * pair + 1) for r in rows_at(place, own_ref, cot_refs, spot_ref)], axis=0
        )
        term = mm(t_ref[:, pair * width : (pair + 1) * width], rows, NN)
        total = term if total is None else total + term
    o_ref[...] = total


def gradient_of(spot, attended, gathered, incoming):
    block = 512
    return pl.pallas_call(
        gradient_kernel,
        grid=(DOUT // block,),
        in_specs=[
            pl.BlockSpec(memory_space=pltpu.SMEM),
            pl.BlockSpec((ZED * HALVES, CHUNK, COLS), lambda i: (0, 0, 0)),
            pl.BlockSpec((ZED, CHUNK, block), lambda i: (0, 0, i)),
        ]
        + [pl.BlockSpec((CHUNK, block), lambda i: (0, i))] * len(ORDER),
        out_specs=pl.BlockSpec((COLS, block), lambda i: (0, i)),
        out_shape=jax.ShapeDtypeStruct((COLS, DOUT), jnp.float32),
        scratch_shapes=[pltpu.VMEM((COLS, TOK), jnp.bfloat16)],
        compiler_params=params(59400000),
        cost_estimate=cost(2 * TOK * COLS * DOUT, 2 * TOK * (COLS + DOUT) + 4 * COLS * DOUT),
        name="weight_gradient",
    )(spot, attended, gathered, *incoming)


def backward_kernel(spot_ref, own_ref, *refs):
    cot_refs, refs = refs[: len(ORDER)], refs[len(ORDER) :]
    w_ref, q_ref, k_ref, v_ref, p_ref, dq_ref, dk_ref, dv_ref, u_ref, ak_ref, av_ref = refs
    head = pl.program_id(0)

    @pl.when(head == 0)
    def _():
        for place in range(0, len(ORDER), 2):
            rows = jnp.concatenate(
                [r for p in (place, place + 1) for r in rows_at(p, own_ref, cot_refs, spot_ref)], axis=0
            )
            rows = mm(rows, w_ref[...], NT).astype(jnp.bfloat16)
            for part in range(2 * HALVES):
                z = lax.rem(spot_ref[0] + ORDER[place + part // HALVES], ZED)
                t = token_block(z, part % HALVES, spot_ref)
                for h in range(COLS // HD):
                    u_ref[h, pl.ds(t * CHUNK, CHUNK), :] = rows[
                        part * CHUNK : (part + 1) * CHUNK, h * HD : (h + 1) * HD
                    ]

    keys_t = k_ref[...].astype(jnp.float32).T.astype(jnp.bfloat16)
    blocks = TOK // QB
    for i in reversed(range(blocks)):
        low, high = i * QB, (i + 1) * QB
        up = u_ref[head, low:high, :]
        chance = p_ref[0, :high, low:high]
        wide = chance.astype(jnp.float32)
        prob_grad = mm(v_ref[:high, :], up, NT)
        center = jnp.sum(wide * prob_grad, axis=0, keepdims=True)
        score_grad = (wide * (prob_grad - center) * SCALE).astype(jnp.bfloat16)
        dq_ref[low:high, :] = mm(keys_t[:, :high], score_grad, NN).T.astype(jnp.bfloat16)
        more_v = mm(chance, up, NN)
        more_k = mm(score_grad, q_ref[low:high, :], NN)
        if i == blocks - 1:
            av_ref[...] = more_v
            ak_ref[...] = more_k
        else:
            av_ref[:high, :] += more_v
            ak_ref[:high, :] += more_k
    dv_ref[...] = av_ref[...].astype(jnp.bfloat16)
    dk_ref[...] = ak_ref[...].astype(jnp.bfloat16)


def backward(spot, gathered, incoming, weight, queries, keys, values, chances):
    heads = COLS // HD
    head_block = pl.BlockSpec((TOK, HD), lambda h: (0, h))
    return pl.pallas_call(
        backward_kernel,
        grid=(heads,),
        in_specs=[
            pl.BlockSpec(memory_space=pltpu.SMEM),
            pl.BlockSpec((ZED, CHUNK, DOUT), lambda h: (0, 0, 0)),
        ]
        + [pl.BlockSpec((CHUNK, DOUT), lambda h: (0, 0))] * len(ORDER)
        + [
            pl.BlockSpec((COLS, DOUT), lambda h: (0, 0)),
            head_block,
            head_block,
            head_block,
            pl.BlockSpec((1, TOK, TOK), lambda h: (h, 0, 0)),
        ],
        out_specs=[head_block] * 3,
        out_shape=[jax.ShapeDtypeStruct((TOK, COLS), jnp.bfloat16)] * 3,
        scratch_shapes=[
            pltpu.VMEM((heads, TOK, HD), jnp.bfloat16),
            pltpu.VMEM((TOK, HD), jnp.float32),
            pltpu.VMEM((TOK, HD), jnp.float32),
        ],
        compiler_params=params(59400000),
        cost_estimate=cost(
            2 * TOK * COLS * DOUT + 8 * TOK * TOK * COLS, 2 * (TOK * DOUT + COLS * DOUT + 6 * TOK * COLS + heads * TOK * TOK)
        ),
        name="attend_backward",
    )(spot, gathered, *incoming, weight, queries, keys, values, chances)


def adam_kernel(w_ref, one_ref, two_ref, g_ref, nw_ref, n1_ref, n2_ref):
    shape = g_ref.shape
    gradient = g_ref[...]
    first_full = 0.9 * one_ref[...].reshape(shape).astype(jnp.float32) + 0.1 * gradient
    second_full = 0.999 * two_ref[...].reshape(shape).astype(jnp.float32) + 0.001 * gradient * gradient
    fix_one = 1.0 - 0.9**ADAM_STEP
    fix_two = 1.0 - 0.999**ADAM_STEP
    spread = second_full * (1.0 / fix_two)
    update = first_full * (0.001 / fix_one) / (spread * lax.rsqrt(spread) + 1e-08)
    nw_ref[...] = (w_ref[...].astype(jnp.float32) - update).astype(jnp.bfloat16)
    n1_ref[...] = first_full.astype(jnp.bfloat16)
    n2_ref[...] = second_full.astype(jnp.bfloat16)


def adam(weight, moments, gradient):
    piece = COLS // MEMBERS
    group = 8
    rows = pl.BlockSpec((group * piece, DOUT), lambda i: (i, 0))
    out = jax.ShapeDtypeStruct((COLS, DOUT), jnp.bfloat16)
    return pl.pallas_call(
        adam_kernel,
        grid=(MEMBERS // group,),
        in_specs=[
            rows,
            pl.BlockSpec((group, piece, DOUT), lambda i: (i, 0, 0)),
            pl.BlockSpec((group, piece, DOUT), lambda i: (i, 1, 0)),
            rows,
        ],
        out_specs=[rows] * 3,
        out_shape=[out] * 3,
        compiler_params=params(59400000),
        cost_estimate=cost(20 * COLS * DOUT, 16 * COLS * DOUT, 3 * COLS * DOUT),
        name="adam",
    )(weight, moments, moments, gradient)


def select_kernel(source_ref, x_ref, *refs):
    o_ref, sems = refs[-2:]
    copies = [
        pltpu.make_async_copy(x_ref.at[source_ref[i]], o_ref.at[i], sems.at[i]) for i in range(MEMBERS)
    ]
    for copy in copies:
        copy.start()
    for copy in copies:
        copy.wait()


def select(source, pieces, after, weighed):
    return pl.pallas_call(
        select_kernel,
        in_specs=[pl.BlockSpec(memory_space=pltpu.SMEM), pl.BlockSpec(memory_space=pltpu.VMEM)]
        + [ANYWHERE] * len(after),
        out_specs=ANYWHERE,
        out_shape=jax.ShapeDtypeStruct(pieces.shape, pieces.dtype),
        scratch_shapes=[pltpu.SemaphoreType.DMA((MEMBERS,))],
        compiler_params=params(),
        cost_estimate=cost(0, weighed * pieces.size),
        name="select_pieces",
    )(source, pieces, *after)


def swap_members(pieces):
    return lax.all_to_all(pieces, "member", split_axis=0, concat_axis=0, tiled=True)


def on_device(
    source, query_rows, key_rows, value_rows, cotangent, out_weight, first_moment, second_moment
):
    queries, keys, values = query_rows[0], key_rows[0], value_rows[0]
    pieces = (MEMBERS, COLS // MEMBERS, DOUT)

    place = lax.axis_index("tp")
    spot = jnp.stack([place % ZED, place // ZED]).astype(jnp.int32)
    own = cotangent[0]
    gathered = lax.all_gather(own, "tp", axis=0, axis_index_groups=Z_GROUPS)
    moments = jnp.concatenate([first_moment.reshape(pieces), second_moment.reshape(pieces)], axis=1)
    attended, chances = forward(spot, queries, keys, values, [])

    other = lax.ppermute(own, "tp", HALF_SWAP)
    weight = swap_members(select(source, swap_members(out_weight.reshape(pieces)), [other, attended, moments], 4)).reshape(COLS, DOUT)
    up, down, incoming = other, other, [other]
    for _ in range(ZED // 2 - 1):
        up = lax.ppermute(up, "tp", ring(1))
        down = lax.ppermute(down, "tp", ring(-1))
        incoming += [up, down]
    split = CHUNK // 2
    across = [lax.ppermute(up[:split], "tp", ring(1)), lax.ppermute(down[split:], "tp", ring(-1))]
    incoming.append(jnp.concatenate(across, axis=0))

    partial = project(attended.reshape(TOK, COLS), weight, incoming[3:5])
    moments = swap_members(select(source, swap_members(moments), incoming[5:], 4))
    gradient = gradient_of(spot, attended, gathered, incoming)
    query_grad, key_grad, value_grad = backward(
        spot, gathered, incoming, weight, queries, keys, values, chances
    )

    summed = lax.psum_scatter(
        partial, "tp", scatter_dimension=0, tiled=True, axis_index_groups=Z_GROUPS
    )
    summed, query_grad, gradient = lax.optimization_barrier((summed, query_grad, gradient))
    theirs = lax.ppermute(summed[CHUNK:], "tp", HALF_SWAP)
    mixture = (summed[:CHUNK].astype(jnp.float32) + theirs.astype(jnp.float32)).astype(jnp.bfloat16)

    new_weight, new_first, new_second = adam(weight, moments, gradient)
    return (
        mixture[None],
        query_grad[None],
        key_grad[None],
        value_grad[None],
        new_weight[None],
        new_first[None],
        new_second[None],
    )


def solution(mesh):
    placed = (
        P(),
        P("member", None, "tp"),
        P("member", None, "tp"),
        P("member", None, "tp"),
        P("member", "tp", None),
        P("member", "tp", None),
        P("member", "tp", None),
        P("member", "tp", None),
    )
    return jax.shard_map(
        on_device,
        mesh=mesh,
        in_specs=placed,
        out_specs=(
            P("member", "tp", None),
            P("member", None, "tp"),
            P("member", None, "tp"),
            P("member", None, "tp"),
            P("member", "tp", None),
            P("member", "tp", None),
            P("member", "tp", None),
        ),
        check_vma=False,
    )
```

```python
import jax
import jax.numpy as jnp
from jax import lax
from jax.experimental import pallas as pl
from jax.experimental.pallas import tpu as pltpu
from jax.sharding import PartitionSpec as P

HD = 128
ADAM_STEP = 100
MEMBERS = 16
ZED = 8
HALVES = 2
TOK = 1024
DOUT = 2560
COLS = 256
PIECE = COLS // MEMBERS
CHUNK = TOK // (ZED * HALVES)
QB = 256
SCALE = HD ** (-0.5)
VMEM_BYTES = 48 * 1024 * 1024
ANYWHERE = pl.BlockSpec(memory_space=pl.ANY)

Z_GROUPS = [[half * ZED + z for z in range(ZED)] for half in range(HALVES)]
ORDER = [0, 7, 1, 6, 2, 5, 3, 4]
HALF_SWAP = [(t, (t + ZED) % (ZED * HALVES)) for t in range(ZED * HALVES)]

NN = (((1,), (0,)), ((), ()))
NT = (((1,), (1,)), ((), ()))


def mm(a, b, dims):
    return lax.dot_general(a, b, dims, preferred_element_type=jnp.float32)


def params(vmem=VMEM_BYTES):
    return pltpu.CompilerParams(vmem_limit_bytes=vmem)


def cost(flops, nbytes, trans=0):
    return pl.CostEstimate(flops=flops, bytes_accessed=nbytes, transcendentals=trans)


def ring(step):
    return [(h * ZED + z, h * ZED + (z + step) % ZED) for h in range(HALVES) for z in range(ZED)]


def token_block(z, part, spot_ref):
    half = spot_ref[1]
    return z + ZED * (half + part - 2 * half * part)


def forward_kernel(spot_ref, q_ref, k_ref, v_ref, *refs):
    att_ref, p_ref = refs[-2:]
    half = spot_ref[1]
    keys = k_ref[...]
    values_t = v_ref[...].astype(jnp.float32).T.astype(jnp.bfloat16)
    row = lax.broadcasted_iota(jnp.int32, (QB, QB), 0)
    col = lax.broadcasted_iota(jnp.int32, (QB, QB), 1)
    visible = row <= col
    for i in range(TOK // QB):
        low, high = i * QB, (i + 1) * QB
        queries = q_ref[low:high, :]
        last = jnp.where(visible, mm(keys[low:high], queries, NT) * SCALE, -1e30)
        top = jnp.max(last, axis=0, keepdims=True)
        if i:
            early = mm(keys[:low], queries, NT) * SCALE
            top = jnp.maximum(top, jnp.max(early, axis=0, keepdims=True))
            early = jnp.exp(early - top)
        last = jnp.exp(last - top)
        total = jnp.sum(last, axis=0, keepdims=True)
        if i:
            total = total + jnp.sum(early, axis=0, keepdims=True)
        inverse = 1.0 / total
        last = (last * inverse).astype(jnp.bfloat16)
        p_ref[0, low:high, low:high] = last
        out_t = mm(values_t[:, low:high], last, NN)
        if i:
            early = (early * inverse).astype(jnp.bfloat16)
            p_ref[0, :low, low:high] = early
            out_t = out_t + mm(values_t[:, :low], early, NN)
        rows = out_t.T.astype(jnp.bfloat16)
        for part in range(QB // CHUNK):
            t = i * (QB // CHUNK) + part
            side = half if t < ZED else 1 - half
            att_ref[(t % ZED) * HALVES + side] = rows[part * CHUNK : (part + 1) * CHUNK]


def forward(spot, queries, keys, values, after):
    heads = COLS // HD
    head_block = pl.BlockSpec((TOK, HD), lambda h: (0, h))
    return pl.pallas_call(
        forward_kernel,
        grid=(heads,),
        in_specs=[pl.BlockSpec(memory_space=pltpu.SMEM)] + [head_block] * 3 + [ANYWHERE] * len(after),
        out_specs=[
            pl.BlockSpec((ZED * HALVES, CHUNK, HD), lambda h: (0, 0, h)),
            pl.BlockSpec((1, TOK, TOK), lambda h: (h, 0, 0)),
        ],
        out_shape=[
            jax.ShapeDtypeStruct((ZED * HALVES, CHUNK, COLS), jnp.bfloat16),
            jax.ShapeDtypeStruct((heads, TOK, TOK), jnp.bfloat16),
        ],
        compiler_params=params(),
        cost_estimate=cost(4 * TOK * TOK * COLS, 8 * TOK * COLS + 2 * heads * TOK * TOK, heads * TOK * TOK),
        name="attend_forward",
    )(spot, queries, keys, values, *after)


def project_kernel(a_ref, w_ref, *refs):
    o_ref = refs[-1]
    o_ref[...] = mm(a_ref[...], w_ref[...], NN).astype(jnp.bfloat16)


def project(attended, weight, after):
    block = 512
    return pl.pallas_call(
        project_kernel,
        grid=(TOK // block,),
        in_specs=[
            pl.BlockSpec((block, COLS), lambda i: (i, 0)),
            pl.BlockSpec((COLS, DOUT), lambda i: (0, 0)),
        ]
        + [ANYWHERE] * len(after),
        out_specs=pl.BlockSpec((block, DOUT), lambda i: (i, 0)),
        out_shape=jax.ShapeDtypeStruct((TOK, DOUT), jnp.bfloat16),
        compiler_params=params(),
        cost_estimate=cost(2 * TOK * COLS * DOUT, 2 * (TOK * COLS + COLS * DOUT + TOK * DOUT)),
        name="project",
    )(attended, weight, *after)


def rows_at(place, own_ref, cot_refs, spot_ref):
    z = lax.rem(spot_ref[0] + ORDER[place], ZED)
    return [own_ref[z], cot_refs[place][...]]


def gradient_kernel(spot_ref, a_ref, own_ref, *refs):
    cot_refs, (o_ref, t_ref) = refs[: len(ORDER)], refs[len(ORDER) :]

    @pl.when(pl.program_id(0) == 0)
    def _():
        for place, offset in enumerate(ORDER):
            z = lax.rem(spot_ref[0] + offset, ZED)
            rows = a_ref[pl.ds(z * HALVES, HALVES)].reshape(HALVES * CHUNK, COLS)
            t_ref[:, place * HALVES * CHUNK : (place + 1) * HALVES * CHUNK] = (
                rows.astype(jnp.float32).T.astype(jnp.bfloat16)
            )

    total = None
    width = 2 * HALVES * CHUNK
    for pair in range(len(ORDER) // 2):
        rows = jnp.concatenate(
            [r for place in (2 * pair, 2 * pair + 1) for r in rows_at(place, own_ref, cot_refs, spot_ref)], axis=0
        )
        term = mm(t_ref[:, pair * width : (pair + 1) * width], rows, NN)
        total = term if total is None else total + term
    o_ref[...] = total


def gradient_of(spot, attended, gathered, incoming):
    block = 512
    return pl.pallas_call(
        gradient_kernel,
        grid=(DOUT // block,),
        in_specs=[
            pl.BlockSpec(memory_space=pltpu.SMEM),
            pl.BlockSpec((ZED * HALVES, CHUNK, COLS), lambda i: (0, 0, 0)),
            pl.BlockSpec((ZED, CHUNK, block), lambda i: (0, 0, i)),
        ]
        + [pl.BlockSpec((CHUNK, block), lambda i: (0, i))] * len(ORDER),
        out_specs=pl.BlockSpec((COLS, block), lambda i: (0, i)),
        out_shape=jax.ShapeDtypeStruct((COLS, DOUT), jnp.float32),
        scratch_shapes=[pltpu.VMEM((COLS, TOK), jnp.bfloat16)],
        compiler_params=params(),
        cost_estimate=cost(2 * TOK * COLS * DOUT, 2 * TOK * (COLS + DOUT) + 4 * COLS * DOUT),
        name="weight_gradient",
    )(spot, attended, gathered, *incoming)


def backward_kernel(spot_ref, own_ref, *refs):
    cot_refs, refs = refs[: len(ORDER)], refs[len(ORDER) :]
    w_ref, q_ref, k_ref, v_ref, p_ref, dq_ref, dk_ref, dv_ref, u_ref, ak_ref, av_ref = refs
    head = pl.program_id(0)

    @pl.when(head == 0)
    def _():
        for place in range(0, len(ORDER), 2):
            rows = jnp.concatenate(
                [r for p in (place, place + 1) for r in rows_at(p, own_ref, cot_refs, spot_ref)], axis=0
            )
            rows = mm(rows, w_ref[...], NT).astype(jnp.bfloat16)
            for part in range(2 * HALVES):
                z = lax.rem(spot_ref[0] + ORDER[place + part // HALVES], ZED)
                t = token_block(z, part % HALVES, spot_ref)
                for h in range(COLS // HD):
                    u_ref[h, pl.ds(t * CHUNK, CHUNK), :] = rows[
                        part * CHUNK : (part + 1) * CHUNK, h * HD : (h + 1) * HD
                    ]

    keys_t = k_ref[...].astype(jnp.float32).T.astype(jnp.bfloat16)
    blocks = TOK // QB
    for i in reversed(range(blocks)):
        low, high = i * QB, (i + 1) * QB
        up = u_ref[head, low:high, :]
        chance = p_ref[0, :high, low:high]
        wide = chance.astype(jnp.float32)
        prob_grad = mm(v_ref[:high, :], up, NT)
        center = jnp.sum(wide * prob_grad, axis=0, keepdims=True)
        score_grad = (wide * (prob_grad - center) * SCALE).astype(jnp.bfloat16)
        dq_ref[low:high, :] = mm(keys_t[:, :high], score_grad, NN).T.astype(jnp.bfloat16)
        more_v = mm(chance, up, NN)
        more_k = mm(score_grad, q_ref[low:high, :], NN)
        if i == blocks - 1:
            av_ref[...] = more_v
            ak_ref[...] = more_k
        else:
            av_ref[:high, :] += more_v
            ak_ref[:high, :] += more_k
    dv_ref[...] = av_ref[...].astype(jnp.bfloat16)
    dk_ref[...] = ak_ref[...].astype(jnp.bfloat16)


def backward(spot, gathered, incoming, weight, queries, keys, values, chances):
    heads = COLS // HD
    head_block = pl.BlockSpec((TOK, HD), lambda h: (0, h))
    return pl.pallas_call(
        backward_kernel,
        grid=(heads,),
        in_specs=[
            pl.BlockSpec(memory_space=pltpu.SMEM),
            pl.BlockSpec((ZED, CHUNK, DOUT), lambda h: (0, 0, 0)),
        ]
        + [pl.BlockSpec((CHUNK, DOUT), lambda h: (0, 0))] * len(ORDER)
        + [
            pl.BlockSpec((COLS, DOUT), lambda h: (0, 0)),
            head_block,
            head_block,
            head_block,
            pl.BlockSpec((1, TOK, TOK), lambda h: (h, 0, 0)),
        ],
        out_specs=[head_block] * 3,
        out_shape=[jax.ShapeDtypeStruct((TOK, COLS), jnp.bfloat16)] * 3,
        scratch_shapes=[
            pltpu.VMEM((heads, TOK, HD), jnp.bfloat16),
            pltpu.VMEM((TOK, HD), jnp.float32),
            pltpu.VMEM((TOK, HD), jnp.float32),
        ],
        compiler_params=params(),
        cost_estimate=cost(
            2 * TOK * COLS * DOUT + 8 * TOK * TOK * COLS, 2 * (TOK * DOUT + COLS * DOUT + 6 * TOK * COLS + heads * TOK * TOK)
        ),
        name="attend_backward",
    )(spot, gathered, *incoming, weight, queries, keys, values, chances)


def adam_kernel(w_ref, one_ref, two_ref, g_ref, nw_ref, n1_ref, n2_ref):
    shape = g_ref.shape
    gradient = g_ref[...]
    first_full = 0.9 * one_ref[...].reshape(shape).astype(jnp.float32) + 0.1 * gradient
    second_full = 0.999 * two_ref[...].reshape(shape).astype(jnp.float32) + 0.001 * gradient * gradient
    fix_one = 1.0 - 0.9**ADAM_STEP
    fix_two = 1.0 - 0.999**ADAM_STEP
    spread = second_full * (1.0 / fix_two)
    update = first_full * (0.001 / fix_one) / (spread * lax.rsqrt(spread) + 1e-08)
    nw_ref[...] = (w_ref[...].astype(jnp.float32) - update).astype(jnp.bfloat16)
    n1_ref[...] = first_full.astype(jnp.bfloat16)
    n2_ref[...] = second_full.astype(jnp.bfloat16)


def adam(weight, moments, gradient):
    piece = COLS // MEMBERS
    group = 8
    rows = pl.BlockSpec((group * piece, DOUT), lambda i: (i, 0))
    out = jax.ShapeDtypeStruct((COLS, DOUT), jnp.bfloat16)
    return pl.pallas_call(
        adam_kernel,
        grid=(MEMBERS // group,),
        in_specs=[
            rows,
            pl.BlockSpec((group, piece, DOUT), lambda i: (i, 0, 0)),
            pl.BlockSpec((group, piece, DOUT), lambda i: (i, 1, 0)),
            rows,
        ],
        out_specs=[rows] * 3,
        out_shape=[out] * 3,
        compiler_params=params(59400000),
        cost_estimate=cost(20 * COLS * DOUT, 16 * COLS * DOUT, 3 * COLS * DOUT),
        name="adam",
    )(weight, moments, moments, gradient)


def select_kernel(source_ref, x_ref, *refs):
    o_ref, sems = refs[-2:]
    rows = pl.ds(pl.multiple_of(pl.program_id(0) * PIECE, PIECE), PIECE)
    copies = [
        pltpu.make_async_copy(x_ref.at[source_ref[i]], o_ref.at[i, rows], sems.at[i]) for i in range(MEMBERS)
    ]
    for copy in copies:
        copy.start()
    for copy in copies:
        copy.wait()


def select(source, pieces, after, weighed, vmem):
    return pl.pallas_call(
        select_kernel,
        grid=(pieces.shape[1] // PIECE,),
        in_specs=[
            pl.BlockSpec(memory_space=pltpu.SMEM),
            pl.BlockSpec((MEMBERS, PIECE, DOUT), lambda i: (0, i, 0)),
        ]
        + [ANYWHERE] * len(after),
        out_specs=ANYWHERE,
        out_shape=jax.ShapeDtypeStruct(pieces.shape, pieces.dtype),
        scratch_shapes=[pltpu.SemaphoreType.DMA((MEMBERS,))],
        compiler_params=params(vmem),
        cost_estimate=cost(0, weighed * pieces.size),
        name="select_pieces",
    )(source, pieces, *after)


def swap_members(pieces):
    return lax.all_to_all(pieces, "member", split_axis=0, concat_axis=0, tiled=True)


def on_device(
    source, query_rows, key_rows, value_rows, cotangent, out_weight, first_moment, second_moment
):
    queries, keys, values = query_rows[0], key_rows[0], value_rows[0]
    pieces = (MEMBERS, COLS // MEMBERS, DOUT)

    place = lax.axis_index("tp")
    spot = jnp.stack([place % ZED, place // ZED]).astype(jnp.int32)
    own = cotangent[0]
    gathered = lax.all_gather(own, "tp", axis=0, axis_index_groups=Z_GROUPS)
    moments = jnp.concatenate([first_moment.reshape(pieces), second_moment.reshape(pieces)], axis=1)
    attended, chances = forward(spot, queries, keys, values, [])

    other = lax.ppermute(own, "tp", HALF_SWAP)
    weight = swap_members(select(source, swap_members(out_weight.reshape(pieces)), [other, attended, moments], 4, VMEM_BYTES)).reshape(COLS, DOUT)
    up, down, incoming = other, other, [other]
    for _ in range(ZED // 2 - 1):
        up = lax.ppermute(up, "tp", ring(1))
        down = lax.ppermute(down, "tp", ring(-1))
        incoming += [up, down]
    split = CHUNK // 2
    across = [lax.ppermute(up[:split], "tp", ring(1)), lax.ppermute(down[split:], "tp", ring(-1))]
    incoming.append(jnp.concatenate(across, axis=0))

    partial = project(attended.reshape(TOK, COLS), weight, incoming[3:5])
    moments = swap_members(select(source, swap_members(moments), incoming[5:], 4, 61500000))
    gradient = gradient_of(spot, attended, gathered, incoming)
    query_grad, key_grad, value_grad = backward(
        spot, gathered, incoming, weight, queries, keys, values, chances
    )

    summed = lax.psum_scatter(
        partial, "tp", scatter_dimension=0, tiled=True, axis_index_groups=Z_GROUPS
    )
    summed, query_grad, gradient = lax.optimization_barrier((summed, query_grad, gradient))
    theirs = lax.ppermute(summed[CHUNK:], "tp", HALF_SWAP)
    mixture = (summed[:CHUNK].astype(jnp.float32) + theirs.astype(jnp.float32)).astype(jnp.bfloat16)

    new_weight, new_first, new_second = adam(weight, moments, gradient)
    return (
        mixture[None],
        query_grad[None],
        key_grad[None],
        value_grad[None],
        new_weight[None],
        new_first[None],
        new_second[None],
    )


def solution(mesh):
    placed = (
        P(),
        P("member", None, "tp"),
        P("member", None, "tp"),
        P("member", None, "tp"),
        P("member", "tp", None),
        P("member", "tp", None),
        P("member", "tp", None),
        P("member", "tp", None),
    )
    return jax.shard_map(
        on_device,
        mesh=mesh,
        in_specs=placed,
        out_specs=(
            P("member", "tp", None),
            P("member", None, "tp"),
            P("member", None, "tp"),
            P("member", None, "tp"),
            P("member", "tp", None),
            P("member", "tp", None),
            P("member", "tp", None),
        ),
        check_vma=False,
    )
```
